32 devices in a mesh: groups: 2 (over y), owner: 4 (over x, core), tensor: 4 (over z).
Axes of the slice: x: 2, y: 2, z: 4, core: 2. Of those that a mesh axis runs over, the one named last changes fastest.
Arguments:
- queries: bfloat16 [256, 8192], P(('groups', 'owner'), 'tensor'), parts along dimension 0, may hold values from -30 to 30
- stored_keys: bfloat16 [256, 192, 1024], P(('groups', 'owner', 'tensor')), parts along dimension 0, may hold values from -17 to 17
- stored_values: bfloat16 [256, 192, 1024], P(('groups', 'owner', 'tensor')), parts along dimension 0, may hold values from -24 to 24
- lengths: int32 [256], P(('groups', 'owner', 'tensor')), parts along dimension 0, may hold values from 2 to 192, as said below
- request_adapter: int32 [256], P(('groups', 'owner')), parts along dimension 0, may hold values from 0 to 31, as said below
- adapter_bank_row: int32 [64], P('groups'), parts along dimension 0, may hold values from 0 to 31, as said below
- output_projection_weight: bfloat16 [8192, 8192], P('tensor'), may hold values from -0.09375 to 0.09375
- adapter_down_weight: float32 [64, 8192, 64], P(('groups', 'owner'), 'tensor'), parts along dimension 0, may hold values from -0.0625 to 0.0625
- adapter_up_weight: float32 [64, 64, 8192], P(('groups', 'owner'), None, 'tensor'), parts along dimension 0, may hold values from -0.75 to 0.75
Outputs:
- layer_output: bfloat16 [256, 8192], P(('groups', 'owner'), 'tensor'), parts along dimension 0
The draws below stay inside these ranges and needn't reach their ends.
There are 2 independent parts, one for each index of `groups`. The reference program is written for one: setup_inputs(seed, part) draws one part's arguments, and reference() takes and returns one part's arrays. A program takes and returns all parts, laid end to end along the dimension named above; an argument that names none is the same for every part. Nothing has to cross between parts.
Inputs may be any that keep to these rules, and one draw needn't show every extreme that they name: `lengths`: one request of the group has exactly 192 valid positions. The 32 requests of one index of owner are rows o * 32 to (o + 1) * 32 - 1. Among them at most 16 have a bank row adapter_bank_row[request_adapter[r]] with the same quotient by 8; for one quotient, the same for all subgroups, exactly 16 do in every subgroup. `adapter_bank_row`: A permutation of the adapters.
All inputs are finite; a program needn't handle non-finite values.
Results may differ from the reference program's by a relative error of at most 0.0055.
Values may be sent and summed in bfloat16 or wider, within the bound.
A program may use at most 192 MiB of HBM per device.

```python
import math
import jax
import jax.numpy as jnp
from jax import lax

HQ = 64
KVH = 8
HEAD = 128
MODEL_WIDTH = 8192
ADAPTER_RANK = 64
LMAX = 192
ADPT_OWN = 8
ATTENTION_WIDTH = 8192
REQ = 32
REQUESTS = 128
CAP = 16
ADAPTER_TOTAL = 32
N_OWNER = 4


def shared_routing(key):
    mapping = jax.random.permutation(jax.random.fold_in(key, 101), ADAPTER_TOTAL).astype(jnp.int32)
    hottest = jax.random.randint(jax.random.fold_in(key, 102), (), 0, N_OWNER)

    def one_group(group_key):
        first_key, second_key, third_key, fourth_key = jax.random.split(group_key, 4)
        others = jax.random.permutation(first_key, (N_OWNER - 1) * CAP)[:REQ - CAP] + CAP
        chosen = jnp.concatenate([jnp.arange(CAP), others])
        chosen = chosen[jax.random.permutation(second_key, REQ)]
        owner_of = (chosen // CAP + hottest) % N_OWNER
        inner = jnp.minimum(jax.random.randint(third_key, (REQ,), 0, ADPT_OWN), jax.random.randint(fourth_key, (REQ,), 0, ADPT_OWN))
        return owner_of * ADPT_OWN + inner
    bank_rows = jax.vmap(one_group)(jax.random.split(jax.random.fold_in(key, 103), N_OWNER))
    inverse = jnp.argsort(mapping)
    chosen_ids = inverse[bank_rows.reshape(-1)].astype(jnp.int32)
    return (mapping, chosen_ids)


def draw_adapter_bank_row(key, part):
    mapping, chosen_ids = shared_routing(key)
    return mapping


def draw_request_adapter(key, part):
    mapping, chosen_ids = shared_routing(key)
    return chosen_ids


def draw_lengths(key, part):
    key = jax.random.fold_in(key, 5)
    first_key, second_key, third_key = jax.random.split(key, 3)
    leading_factor = jax.random.randint(first_key, (REQUESTS,), 0, LMAX - 1)
    trailing_factor = jax.random.randint(second_key, (REQUESTS,), 0, LMAX - 1)
    picked = jax.random.randint(third_key, (), 0, REQUESTS)
    spans = 2 + jnp.maximum(leading_factor, trailing_factor)
    return jnp.where(jnp.arange(REQUESTS) == picked, LMAX, spans).astype(jnp.int32)


def draw_queries(key, part):
    key = jax.random.fold_in(key, 7)
    group_size = HQ // KVH
    values = jnp.clip(jax.random.normal(key, (REQUESTS, KVH, group_size, HEAD), jnp.float32), -5.0, 5.0)
    return values.reshape(REQUESTS, HQ * HEAD).astype(jnp.bfloat16)


def draw_stored_keys(key, part):
    key = jax.random.fold_in(key, 9)
    values = jnp.clip(jax.random.normal(key, (REQUESTS, LMAX, KVH, HEAD), jnp.float32), -5.0, 5.0)
    return values.reshape(REQUESTS, LMAX, KVH * HEAD).astype(jnp.bfloat16)


def raised(array, own_key, source, target, blocks, factor):
    def block_of(dim):
        return (jnp.arange(array.shape[dim]) // (array.shape[dim] // blocks)).reshape((-1,) + (1,) * (array.ndim - 1 - dim))

    one_side = jax.random.permutation(own_key, blocks)[block_of(target)]
    far = (block_of(target) + blocks // 2) % blocks
    return jnp.where((block_of(source) == one_side) | (block_of(source) == far), factor * array, array)


def block_scale(own_key, shape, cuts, low, high):
    def one(position, parts):
        heights = jax.random.uniform(jax.random.fold_in(jax.random.fold_in(own_key, 6), position), (parts,), jnp.float32, low / len(cuts), high / len(cuts))
        return jnp.repeat(jnp.exp(heights), shape[position] // parts).reshape((-1,) + (1,) * (len(shape) - position - 1))

    factor_of = one(*cuts[0])
    for cut in cuts[1:]:
        factor_of = factor_of * one(*cut)
    return factor_of


def normal_values(stream_key, extent, spread, most, cuts=(), held_as=jnp.bfloat16):
    loudness = block_scale(stream_key, extent, cuts, -0.22, 0.18) if cuts else 1.0
    values = jax.random.normal(stream_key, extent, jnp.float32) * spread * loudness
    return jnp.minimum(jnp.maximum(values, -most), most).astype(held_as)


def noise_with(stream_key, extent, spread, most, pieces, heavy, dtype=jnp.bfloat16):
    array = spread * jax.random.normal(stream_key, extent, jnp.float32)
    if pieces:
        array = array * block_scale(stream_key, extent, pieces, -0.22, 0.18)
    return jnp.clip(raised(array, jax.random.fold_in(stream_key, 3), *heavy), -most, most).astype(dtype)


def setup_inputs(seed: int = 0, part: int = 0) -> dict:
    seeds = jax.random.split(jax.random.key(seed), 10)
    own_keys = jax.random.split(jax.random.fold_in(seeds[9], part), 10)
    queries = draw_queries(jax.random.fold_in(jax.random.fold_in(seeds[9], part), 71), part)
    stored_keys = draw_stored_keys(jax.random.fold_in(jax.random.fold_in(seeds[9], part), 71), part)
    stored_values = normal_values(own_keys[2], (REQUESTS, LMAX, KVH * HEAD), 4.0, 24.0, ((0, 16),))
    lengths = draw_lengths(jax.random.fold_in(jax.random.fold_in(seeds[9], part), 71), part)
    request_adapter = draw_request_adapter(jax.random.fold_in(jax.random.fold_in(seeds[9], part), 71), part)
    adapter_bank_row = draw_adapter_bank_row(jax.random.fold_in(jax.random.fold_in(seeds[9], part), 71), part)
    output_projection_weight = noise_with(seeds[6], (ATTENTION_WIDTH, MODEL_WIDTH), ATTENTION_WIDTH ** -0.5, 0.09375, ((0, 4),), (0, 1, 4, 2.0))
    adapter_down_weight = normal_values(own_keys[7], (ADAPTER_TOTAL, ATTENTION_WIDTH, ADAPTER_RANK), ATTENTION_WIDTH ** -0.5, 0.0625, ((0, 4), (1, 4)), jnp.float32)
    adapter_up_weight = normal_values(own_keys[8], (ADAPTER_TOTAL, ADAPTER_RANK, MODEL_WIDTH), ADAPTER_RANK ** -0.5, 0.75, ((0, 4), (2, 4)), jnp.float32)
    return {"queries": queries, "stored_keys": stored_keys, "stored_values": stored_values, "lengths": lengths, "request_adapter": request_adapter, "adapter_bank_row": adapter_bank_row, "output_projection_weight": output_projection_weight, "adapter_down_weight": adapter_down_weight, "adapter_up_weight": adapter_up_weight}


def attend_group(block):
    query_block, key_block, value_block, length_block = block
    group_size = HQ // KVH
    query_heads = query_block.astype(jnp.float32).reshape(REQ, KVH, group_size, HEAD)
    key_heads = key_block.astype(jnp.float32).reshape(REQ, LMAX, KVH, HEAD)
    value_heads = value_block.astype(jnp.float32).reshape(REQ, LMAX, KVH, HEAD)
    scores = jnp.einsum('rgjd,rpgd->rgjp', query_heads, key_heads) * (1.0 / math.sqrt(HEAD))
    valid = (jnp.arange(LMAX)[None, :] < length_block[:, None])[:, None, None, :]
    scores = jnp.where(valid, scores, -1e+30)
    highest = lax.optimization_barrier(jnp.max(scores, axis=-1, keepdims=True))
    expo = jnp.where(valid, jnp.exp(scores - highest), 0.0)
    total = lax.optimization_barrier(jnp.sum(expo, axis=-1, keepdims=True))
    weights = expo.astype(jnp.bfloat16)
    mixed = jnp.einsum('rgjp,rpgd->rgjd', weights.astype(jnp.float32), value_heads)
    return (mixed / total).astype(jnp.bfloat16).reshape(REQ, HQ * HEAD)

def reference(queries, stored_keys, stored_values, lengths, request_adapter, adapter_bank_row, output_projection_weight, adapter_down_weight, adapter_up_weight):
    owners = REQUESTS // REQ
    blocks = (queries.reshape(owners, REQ, HQ * HEAD), stored_keys.reshape(owners, REQ, LMAX, KVH * HEAD), stored_values.reshape(owners, REQ, LMAX, KVH * HEAD), lengths.reshape(owners, REQ))
    attended = lax.map(attend_group, blocks).reshape(REQUESTS, HQ * HEAD)
    base = jnp.dot(attended, output_projection_weight, preferred_element_type=jnp.float32)
    bank_row = adapter_bank_row[request_adapter].astype(jnp.int32)

    def adapt_one(item):
        vector, request_row_index = item
        leading_factor = lax.dynamic_index_in_dim(adapter_down_weight, request_row_index, 0, keepdims=False)
        trailing_factor = lax.dynamic_index_in_dim(adapter_up_weight, request_row_index, 0, keepdims=False)
        down = jnp.dot(vector.astype(jnp.float32), leading_factor, precision=lax.Precision.HIGHEST)
        return jnp.dot(down, trailing_factor, precision=lax.Precision.HIGHEST)
    lifted = lax.map(adapt_one, (attended, bank_row))
    return (base + lifted).astype(jnp.bfloat16)
```

```python
import functools
import math

import jax
import jax.numpy as jnp
from jax import lax
from jax.experimental import pallas as pl
from jax.experimental.pallas import tpu as pltpu
from jax.sharding import PartitionSpec as P

HQ = 64
KVH = 8
HEAD = 128
F32 = jnp.float32
BF16 = jnp.bfloat16
NT = (((1,), (1,)), ((), ()))


def kernel(
    T, O, CAP, TN,
    q_ref, len_ref, ra_ref, abr_ref, k_hbm, v_hbm, w_hbm, d_hbm, u_hbm,
    out_ref,
    kv_k, kv_v, w_v, d_f, u_f, d_b, u_b,
    qs, qr, qf, attf, atts, attr, xf, xb,
    sel_t, disp, grecv, ds, dr, rs, rr, ps, pr, own,
    lk, lv, lw, ld, lu,
    s_q, r_q, s_a, r_a, s_g, r_g, s_d, r_d, s_r, r_r, s_p, r_p,
):
    me = lax.axis_index("tensor")
    mo = lax.axis_index("owner")
    R, KB = q_ref.shape
    CB = out_ref.shape[1]
    NR = k_hbm.shape[0]
    POS = k_hbm.shape[1]
    HT = HQ // T
    AO, RANK = u_hbm.shape[0], u_hbm.shape[1]
    OC = O * CAP
    far = [(T // 2 + i) % T for i in range(T) if (T // 2 + i) % T != 0]

    loads_k, loads_v = [], []
    for r in range(NR):
        loads_k.append(pltpu.make_async_copy(k_hbm.at[r], kv_k.at[r], lk.at[r]))
        loads_v.append(pltpu.make_async_copy(v_hbm.at[r], kv_v.at[r], lv.at[r]))
        loads_k[r].start()
        loads_v[r].start()
    load_d = pltpu.make_async_copy(d_hbm, d_f, ld)
    load_u = pltpu.make_async_copy(u_hbm, u_f, lu)
    load_d.start()
    load_u.start()
    loads_w = {}
    for k in far + [0]:
        to = lax.rem(me + k, T)
        loads_w[k] = pltpu.make_async_copy(
            w_hbm.at[:, pl.ds(pl.multiple_of(to * CB, CB), CB)], w_v.at[k], lw.at[k]
        )
        loads_w[k].start()

    barrier = pltpu.get_barrier_semaphore()
    for k in range(1, T):
        pl.semaphore_signal(barrier, inc=1, device_id={"tensor": lax.rem(me + k, T)})
    for k in range(1, O):
        pl.semaphore_signal(barrier, inc=1, device_id={"owner": lax.rem(mo + k, O)})

    for t in range(T):
        rows = q_ref[t * NR:(t + 1) * NR, :].astype(F32)
        qs[t] = jnp.concatenate(
            [rows[:, h * HEAD:(h + 1) * HEAD] for h in range(HT)], axis=0
        ).astype(BF16)
    pl.semaphore_wait(barrier, T + O - 2)

    def to_tensor(k, src, dst, ss, rs_):
        c = pltpu.make_async_remote_copy(
            src_ref=src, dst_ref=dst, send_sem=ss.at[k], recv_sem=rs_.at[k],
            device_id={"tensor": lax.rem(me + k, T)},
        )
        c.start()
        return c

    def to_owner(k, target, src, dst, ss, rs_):
        c = pltpu.make_async_remote_copy(
            src_ref=src, dst_ref=dst, send_sem=ss.at[k], recv_sem=rs_.at[k],
            device_id={"owner": target},
        )
        c.start()
        return c

    sent = []
    cq = [to_tensor(k, qs.at[lax.rem(me + k, T)], qr.at[me], s_q, r_q) for k in far]
    sent += cq
    qr[me] = qs[me]

    A = abr_ref.shape[1]
    ia = lax.broadcasted_iota(jnp.int32, (A, A), 0)
    la = lax.broadcasted_iota(jnp.int32, (A, A), 1)
    abr_col = jnp.sum(jnp.where(ia == la, abr_ref[...], 0), axis=1, keepdims=True)
    hits = lax.broadcasted_iota(jnp.int32, (A, R), 0) == ra_ref[...]
    bank = jnp.sum(jnp.where(hits, abr_col, 0), axis=0, keepdims=True)
    who = bank // AO
    inner = bank - who * AO
    OP = max(8, O)
    eq = (lax.broadcasted_iota(jnp.int32, (OP, R), 0) == who).astype(F32)
    ir = lax.broadcasted_iota(jnp.int32, (R, R), 0)
    lr = lax.broadcasted_iota(jnp.int32, (R, R), 1)
    before = jnp.dot(
        eq.astype(BF16), (ir < lr).astype(F32).astype(BF16), preferred_element_type=F32
    )
    rank = jnp.sum(eq * before, axis=0, keepdims=True).astype(jnp.int32)
    place = who * CAP + rank
    sel = (lax.broadcasted_iota(jnp.int32, (OC, R), 0) == place).astype(F32).astype(BF16)
    place_col = jnp.sum(jnp.where(ir == lr, place, 0), axis=1, keepdims=True)
    sel_t[...] = (
        (lax.broadcasted_iota(jnp.int32, (R, OC), 1) == place_col).astype(F32).astype(BF16)
    )
    inner_t = (lax.broadcasted_iota(jnp.int32, (128, R), 0) == inner).astype(F32).astype(BF16)
    marks = lax.dot_general(sel, inner_t, NT, preferred_element_type=F32).astype(BF16)
    for o in range(O):
        disp[o, :, KB:] = marks[o * CAP:(o + 1) * CAP, :]

    for c in cq:
        c.wait_recv()
    for t in range(T):
        qf[t * HT * NR:(t + 1) * HT * NR, :] = qr[t].astype(F32)

    G = HQ // KVH
    head_of = lax.broadcasted_iota(jnp.int32, (HQ, KVH * HEAD), 0) // G
    lane_of = lax.broadcasted_iota(jnp.int32, (HQ, KVH * HEAD), 1) // HEAD
    diagonal = head_of == lane_of
    pos = lax.broadcasted_iota(jnp.int32, (HQ, POS), 1)
    for r in range(NR):
        q_r = qf[pl.ds(r, HQ, stride=NR), :]
        wide = jnp.where(diagonal, jnp.concatenate([q_r] * KVH, axis=1), 0.0).astype(BF16)
        loads_k[r].wait()
        scores = lax.dot_general(wide, kv_k[r], NT, preferred_element_type=F32)
        scores = scores * (1.0 / math.sqrt(HEAD))
        valid = pos < len_ref[r]
        scores = jnp.where(valid, scores, -1e30)
        highest = jnp.max(scores, axis=1, keepdims=True)
        expo = jnp.where(valid, jnp.exp(scores - highest), 0.0)
        total = jnp.sum(expo, axis=1, keepdims=True)
        loads_v[r].wait()
        mixed = jnp.dot(expo.astype(BF16), kv_v[r], preferred_element_type=F32)
        mixed = jnp.concatenate(
            [mixed[g * G:(g + 1) * G, g * HEAD:(g + 1) * HEAD] for g in range(KVH)], axis=0
        )
        attf[pl.ds(r, HQ, stride=NR), :] = mixed / total
    for t in range(T):
        atts[t] = attf[t * HT * NR:(t + 1) * HT * NR, :].astype(BF16)
    ca = [to_tensor(k, atts.at[lax.rem(me + k, T)], attr.at[me], s_a, r_a) for k in far]
    sent += ca
    attr[me] = atts[me]

    load_d.wait()
    load_u.wait()

    @pl.loop(0, AO)
    def _(a):
        rows = pl.ds(pl.multiple_of(a * RANK, RANK), RANK)
        d_b[rows, :] = d_f[a].astype(BF16)
        u_b[rows, :] = u_f[a].astype(BF16)

    for c in ca:
        c.wait_recv()
    for t in range(T):
        got = attr[t].astype(F32)
        for h in range(HT):
            xf[t * NR:(t + 1) * NR, h * HEAD:(h + 1) * HEAD] = got[h * NR:(h + 1) * NR, :]
    xb[...] = xf[...].astype(BF16)

    disp_rows = jnp.dot(sel, xb[...], preferred_element_type=F32).astype(BF16)
    for o in range(O):
        disp[o, :, :KB] = disp_rows[o * CAP:(o + 1) * CAP, :]
    cg = []
    for k in range(1, O):
        o = lax.rem(mo + k, O)
        cg.append(to_owner(k, o, disp.at[o], grecv.at[mo], s_g, r_g))
    sent += cg
    grecv[mo] = disp[mo]

    def project(k):
        loads_w[k].wait()

        @pl.loop(0, CB // TN)
        def _(j):
            cols = pl.ds(pl.multiple_of(j * TN, TN), TN)
            part = jnp.dot(xb[...], w_v[k, :, cols], preferred_element_type=F32)
            if k:
                ps[k, :, cols] = part.astype(BF16)
            else:
                own[:, cols] = part

    cp = []

    def project_and_send(k):
        project(k)
        cp.append(to_tensor(k, ps.at[k], pr.at[me], s_p, r_p))

    half = max(1, len(far) // 3)
    for k in far[:half]:
        project_and_send(k)

    for c in cg:
        c.wait_recv()
    rows_in = grecv[...].reshape(OC, KB + 128)
    ej = lax.broadcasted_iota(jnp.int32, (128, AO * RANK), 0)
    el = lax.broadcasted_iota(jnp.int32, (128, AO * RANK), 1) // RANK
    spread = (ej == el).astype(F32).astype(BF16)
    mask = jnp.dot(rows_in[:, KB:], spread, preferred_element_type=F32)
    every = lax.dot_general(rows_in[:, :KB], d_b[...], NT, preferred_element_type=F32) * mask
    lanes = every[:, :128]
    for i in range(1, AO * RANK // 128):
        lanes = lanes + every[:, i * 128:(i + 1) * 128]
    down = lanes[:, :RANK] + lanes[:, RANK:]
    ds[...] = jnp.concatenate([down[:OC // 2], down[OC // 2:]], axis=1)
    cd = [to_tensor(k, ds, dr.at[me], s_d, r_d) for k in far]
    sent += cd

    for k in far[half:]:
        project_and_send(k)
    sent += cp

    for c in cd:
        c.wait_recv()
    total_down = ds[...]
    for k in range(1, T):
        total_down = total_down + dr[lax.rem(me + k, T)]
    down = jnp.concatenate([total_down[:, :RANK], total_down[:, RANK:]], axis=0)
    twice = jnp.concatenate([down, down], axis=1)
    lifted_in = (jnp.concatenate([twice] * (AO * RANK // 128), axis=1) * mask).astype(BF16)
    lifted = jnp.dot(lifted_in, u_b[...], preferred_element_type=F32).astype(BF16)
    for o in range(O):
        rs[o] = lifted[o * CAP:(o + 1) * CAP, :]
    cr = []
    for k in range(1, O):
        o = lax.rem(mo + k, O)
        cr.append(to_owner(k, o, rs.at[o], rr.at[mo], s_r, r_r))
    sent += cr
    rr[mo] = rs[mo]

    project(0)
    for c in cp:
        c.wait_recv()
    for c in cr:
        c.wait_recv()
    step = min(512, CB)
    for j in range(CB // step):
        cols = slice(j * step, (j + 1) * step)
        whole = jnp.dot(
            sel_t[...], rr[:, :, cols].reshape(OC, step), preferred_element_type=F32
        )
        base = own[:, cols]
        for k in range(1, T):
            base = base + pr[lax.rem(me + k, T), :, cols].astype(F32)
        out_ref[:, cols] = (base + whole).astype(BF16)
    for c in sent:
        c.wait_send()


def local(mesh, q, k, v, lengths, ra, abr, w, d, u):
    T, O = mesh.shape["tensor"], mesh.shape["owner"]
    R, KB = q.shape
    NR, POS, KW = k.shape
    AO, RANK, CB = u.shape
    CAP = 2 * R // O
    OC = O * CAP
    HT = HQ // T
    TN = min(512, CB)
    vm = pltpu.VMEM
    dma = pltpu.SemaphoreType.DMA
    scratch = [
        vm((NR, POS, KW), BF16), vm((NR, POS, KW), BF16),
        vm((T, KB, CB), BF16),
        vm((AO, RANK, KB), F32), vm((AO, RANK, CB), F32),
        vm((AO * RANK, KB), BF16), vm((AO * RANK, CB), BF16),
        vm((T, HT * NR, HEAD), BF16), vm((T, HT * NR, HEAD), BF16), vm((HQ * NR, HEAD), F32),
        vm((HQ * NR, HEAD), F32), vm((T, HT * NR, HEAD), BF16), vm((T, HT * NR, HEAD), BF16),
        vm((R, KB), F32), vm((R, KB), BF16),
        vm((R, OC), BF16), vm((O, CAP, KB + 128), BF16), vm((O, CAP, KB + 128), BF16),
        vm((OC // 2, 2 * RANK), F32), vm((T, OC // 2, 2 * RANK), F32),
        vm((O, CAP, CB), BF16), vm((O, CAP, CB), BF16),
        vm((T, R, CB), BF16), vm((T, R, CB), BF16), vm((R, CB), F32),
        dma((NR,)), dma((NR,)), dma((T,)), dma(()), dma(()),
        dma((T,)), dma((T,)), dma((T,)), dma((T,)), dma((O,)), dma((O,)),
        dma((T,)), dma((T,)), dma((O,)), dma((O,)), dma((T,)), dma((T,)),
    ]
    any_spec = pl.BlockSpec(memory_space=pl.ANY)
    vmem_spec = pl.BlockSpec(memory_space=pltpu.VMEM)
    smem_spec = pl.BlockSpec(memory_space=pltpu.SMEM)
    return pl.pallas_call(
        functools.partial(kernel, T, O, CAP, TN),
        out_shape=jax.ShapeDtypeStruct((R, CB), BF16),
        in_specs=[vmem_spec, smem_spec, vmem_spec, vmem_spec] + [any_spec] * 5,
        out_specs=vmem_spec,
        scratch_shapes=scratch,
        compiler_params=pltpu.CompilerParams(
            collective_id=0, has_side_effects=True, vmem_limit_bytes=60 * 2**20
        ),
        name="attend_project_adapt",
    )(q, lengths, ra.reshape(1, -1), abr.reshape(1, -1), k, v, w, jnp.swapaxes(d, 1, 2), u)


def solution(mesh):
    return jax.shard_map(
        functools.partial(local, mesh),
        mesh=mesh,
        in_specs=(
            P(("groups", "owner"), "tensor"),
            P(("groups", "owner", "tensor"), None, None),
            P(("groups", "owner", "tensor"), None, None),
            P(("groups", "owner", "tensor")),
            P(("groups", "owner")),
            P("groups"),
            P("tensor", None),
            P(("groups", "owner"), "tensor", None),
            P(("groups", "owner"), None, "tensor"),
        ),
        out_specs=P(("groups", "owner"), "tensor"),
        check_vma=False,
    )
```

```python
import functools
import math

import jax
import jax.numpy as jnp
from jax import lax
from jax.experimental import pallas as pl
from jax.experimental.pallas import tpu as pltpu
from jax.sharding import PartitionSpec as P

HQ = 64
KVH = 8
HEAD = 128
F32 = jnp.float32
BF16 = jnp.bfloat16
NT = (((1,), (1,)), ((), ()))


def kernel(
    T, O, CAP, TN,
    q_ref, len_ref, ra_ref, abr_ref, k_hbm, v_hbm, w_hbm, d_hbm, u_hbm,
    out_ref,
    kv_k, kv_v, w_v, d_f, u_f, d_b, u_b,
    qs, qr, qf, attf, atts, attr, xf, xb,
    sel_t, disp, grecv, ds, dr, rs, rr, ps, pr, own, passing,
    lk, lv, lw, ld, lu,
    s_q, r_q, s_a, r_a, s_g, r_g, s_d, r_d, s_r, r_r, s_p, r_p,
):
    me = lax.axis_index("tensor")
    mo = lax.axis_index("owner")
    R, KB = q_ref.shape
    CB = out_ref.shape[1]
    NR = k_hbm.shape[0]
    POS = k_hbm.shape[1]
    HT = HQ // T
    AO, RANK = u_hbm.shape[0], u_hbm.shape[1]
    OC = O * CAP
    far = [(T // 2 + i) % T for i in range(T) if (T // 2 + i) % T != 0]

    loads_k, loads_v = [], []
    for r in range(NR):
        loads_k.append(pltpu.make_async_copy(k_hbm.at[r], kv_k.at[r], lk.at[r]))
        loads_v.append(pltpu.make_async_copy(v_hbm.at[r], kv_v.at[r], lv.at[r]))
        loads_k[r].start()
        loads_v[r].start()
    load_d = pltpu.make_async_copy(d_hbm, d_f, ld)
    load_u = pltpu.make_async_copy(u_hbm, u_f, lu)
    load_d.start()
    load_u.start()
    pair = me + 1 - 2 * lax.rem(me, 2)
    across = lax.rem(me + 2, T)
    if T == 4:
        blocks = [lax.rem(pair + 2, T), across, pair, me]
    else:
        blocks = [lax.rem(me + k, T) for k in far] + [me]
    loads_w = []
    for i, to in enumerate(blocks):
        loads_w.append(pltpu.make_async_copy(
            w_hbm.at[:, pl.ds(pl.multiple_of(to * CB, CB), CB)], w_v.at[i], lw.at[i]
        ))
        loads_w[i].start()

    barrier = pltpu.get_barrier_semaphore()
    for k in range(1, T):
        pl.semaphore_signal(barrier, inc=1, device_id={"tensor": lax.rem(me + k, T)})
    for k in range(1, O):
        pl.semaphore_signal(barrier, inc=1, device_id={"owner": lax.rem(mo + k, O)})

    for t in range(T):
        rows = q_ref[t * NR:(t + 1) * NR, :].astype(F32)
        qs[t] = jnp.concatenate(
            [rows[:, h * HEAD:(h + 1) * HEAD] for h in range(HT)], axis=0
        ).astype(BF16)
    pl.semaphore_wait(barrier, T + O - 2)

    def to_device(i, target, src, dst, ss, rs_):
        c = pltpu.make_async_remote_copy(
            src_ref=src, dst_ref=dst, send_sem=ss.at[i], recv_sem=rs_.at[i],
            device_id={"tensor": target},
        )
        c.start()
        return c

    def to_tensor(k, src, dst, ss, rs_):
        return to_device(k, lax.rem(me + k, T), src, dst, ss, rs_)

    def to_owner(k, target, src, dst, ss, rs_):
        c = pltpu.make_async_remote_copy(
            src_ref=src, dst_ref=dst, send_sem=ss.at[k], recv_sem=rs_.at[k],
            device_id={"owner": target},
        )
        c.start()
        return c

    sent = []
    near = sorted(range(1, T), key=lambda k: min(k, T - k))
    cq = {k: to_tensor(k, qs.at[lax.rem(me + k, T)], qr.at[me], s_q, r_q) for k in near}
    sent += cq.values()
    qr[me] = qs[me]

    A = abr_ref.shape[1]
    ia = lax.broadcasted_iota(jnp.int32, (A, A), 0)
    la = lax.broadcasted_iota(jnp.int32, (A, A), 1)
    abr_col = jnp.sum(jnp.where(ia == la, abr_ref[...], 0), axis=1, keepdims=True)
    hits = lax.broadcasted_iota(jnp.int32, (A, R), 0) == ra_ref[...]
    bank = jnp.sum(jnp.where(hits, abr_col, 0), axis=0, keepdims=True)
    who = bank // AO
    inner = bank - who * AO
    OP = max(8, O)
    eq = (lax.broadcasted_iota(jnp.int32, (OP, R), 0) == who).astype(F32)
    ir = lax.broadcasted_iota(jnp.int32, (R, R), 0)
    lr = lax.broadcasted_iota(jnp.int32, (R, R), 1)
    before = jnp.dot(
        eq.astype(BF16), (ir < lr).astype(F32).astype(BF16), preferred_element_type=F32
    )
    rank = jnp.sum(eq * before, axis=0, keepdims=True).astype(jnp.int32)
    place = who * CAP + rank
    sel = (lax.broadcasted_iota(jnp.int32, (OC, R), 0) == place).astype(F32).astype(BF16)
    place_col = jnp.sum(jnp.where(ir == lr, place, 0), axis=1, keepdims=True)
    sel_t[...] = (
        (lax.broadcasted_iota(jnp.int32, (R, OC), 1) == place_col).astype(F32).astype(BF16)
    )
    inner_t = (lax.broadcasted_iota(jnp.int32, (128, R), 0) == inner).astype(F32).astype(BF16)
    marks = lax.dot_general(sel, inner_t, NT, preferred_element_type=F32).astype(BF16)
    for o in range(O):
        disp[o, :, KB:] = marks[o * CAP:(o + 1) * CAP, :]

    G = HQ // KVH
    for c in loads_k + loads_v:
        c.wait()
    KH = max(1, KVH // T)
    rows_of = KH * G
    head_of = lax.broadcasted_iota(jnp.int32, (rows_of, KH * HEAD), 0) // G
    lane_of = lax.broadcasted_iota(jnp.int32, (rows_of, KH * HEAD), 1) // HEAD
    diagonal = head_of == lane_of
    pos = lax.broadcasted_iota(jnp.int32, (rows_of, POS), 1)
    valid = [pos < len_ref[r] for r in range(NR)]
    valid_all = jnp.concatenate(valid, axis=0)

    def attend(first_row, columns):
        scores = []
        for r in range(NR):
            q_r = qf[pl.ds(first_row + r, rows_of, stride=NR), :]
            wide = jnp.where(diagonal, jnp.concatenate([q_r] * KH, axis=1), 0.0).astype(BF16)
            scores.append(
                lax.dot_general(wide, kv_k[r, :, columns], NT, preferred_element_type=F32)
            )
        scores = jnp.concatenate(scores, axis=0) * (1.0 / math.sqrt(HEAD))
        scores = jnp.where(valid_all, scores, -1e30)
        highest = jnp.max(scores, axis=1, keepdims=True)
        expo = jnp.where(valid_all, jnp.exp(scores - highest), 0.0)
        total = jnp.sum(expo, axis=1, keepdims=True)
        weights = expo.astype(BF16)
        for r in range(NR):
            rows = slice(r * rows_of, (r + 1) * rows_of)
            mixed = jnp.dot(weights[rows], kv_v[r, :, columns], preferred_element_type=F32)
            mixed = jnp.concatenate(
                [mixed[g * G:(g + 1) * G, g * HEAD:(g + 1) * HEAD] for g in range(KH)], axis=0
            )
            attf[pl.ds(first_row + r, rows_of, stride=NR), :] = mixed / total[rows]

    BR = HT * NR
    ca = []
    if KVH % T == 0:
        for k in [0] + near:
            d = lax.rem(me + k, T)
            if k:
                cq[T - k].wait_recv()
            first = pl.multiple_of(d * BR, BR)
            qf[pl.ds(first, BR), :] = qr[d].astype(F32)
            attend(first, pl.ds(pl.multiple_of(d * KH * HEAD, KH * HEAD), KH * HEAD))
            atts[d] = attf[pl.ds(first, BR), :].astype(BF16)
            if k:
                ca.append(to_tensor(k, atts.at[d], attr.at[me], s_a, r_a))
    else:
        for c in cq.values():
            c.wait_recv()
        for t in range(T):
            qf[t * BR:(t + 1) * BR, :] = qr[t].astype(F32)
        for g in range(KVH):
            attend(g * G * NR, slice(g * HEAD, (g + 1) * HEAD))
        for t in range(T):
            atts[t] = attf[t * BR:(t + 1) * BR, :].astype(BF16)
        ca = [to_tensor(k, atts.at[lax.rem(me + k, T)], attr.at[me], s_a, r_a) for k in far]
    sent += ca
    attr[me] = atts[me]

    load_d.wait()
    load_u.wait()

    @pl.loop(0, AO)
    def _(a):
        rows = pl.ds(pl.multiple_of(a * RANK, RANK), RANK)
        d_b[rows, :] = d_f[a].astype(BF16)
        u_b[rows, :] = u_f[a].astype(BF16)

    for c in ca:
        c.wait_recv()
    for t in range(T):
        got = attr[t].astype(F32)
        for h in range(HT):
            xf[t * NR:(t + 1) * NR, h * HEAD:(h + 1) * HEAD] = got[h * NR:(h + 1) * NR, :]
    xb[...] = xf[...].astype(BF16)

    disp_rows = jnp.dot(sel, xb[...], preferred_element_type=F32).astype(BF16)
    for o in range(O):
        disp[o, :, :KB] = disp_rows[o * CAP:(o + 1) * CAP, :]
    cg = []
    for k in range(1, O):
        o = lax.rem(mo + k, O)
        cg.append(to_owner(k, o, disp.at[o], grecv.at[mo], s_g, r_g))
    sent += cg
    grecv[mo] = disp[mo]

    HB = CB // 2

    def project(i, h, out):
        if h == 0:
            loads_w[i].wait()

        @pl.loop(0, HB // TN)
        def _(j):
            cols = pl.ds(pl.multiple_of(h * HB + j * TN, TN), TN)
            part = jnp.dot(xb[...], w_v[i, :, cols], preferred_element_type=F32)
            out[:, cols] = part.astype(out.dtype)

    def half_of(h):
        return slice(h * HB, (h + 1) * HB)

    def send_sum(i, h, target, slot):
        return to_device(
            2 * i + h, target, ps.at[i, :, half_of(h)], pr.at[slot, :, half_of(h)], s_p, r_p
        )

    cp = []
    if T == 4:
        for h in range(2):
            project(0, h, ps.at[0])
            cp.append(send_sum(0, h, pair, 0))
        for h in range(2):
            project(1, h, passing)
    else:
        half = len(far) // 3
        for i in range(half):
            for h in range(2):
                project(i, h, ps.at[i])
                cp.append(send_sum(i, h, blocks[i], me))

    for c in cg:
        c.wait_recv()
    rows_in = grecv[...].reshape(OC, KB + 128)
    ej = lax.broadcasted_iota(jnp.int32, (128, AO * RANK), 0)
    el = lax.broadcasted_iota(jnp.int32, (128, AO * RANK), 1) // RANK
    spread = (ej == el).astype(F32).astype(BF16)
    mask = jnp.dot(rows_in[:, KB:], spread, preferred_element_type=F32)
    every = lax.dot_general(rows_in[:, :KB], d_b[...], NT, preferred_element_type=F32) * mask
    lanes = every[:, :128]
    for i in range(1, AO * RANK // 128):
        lanes = lanes + every[:, i * 128:(i + 1) * 128]
    down = lanes[:, :RANK] + lanes[:, RANK:]
    ds[...] = jnp.concatenate([down[:OC // 2], down[OC // 2:]], axis=1)
    cd = [to_tensor(k, ds, dr.at[me], s_d, r_d) for k in far]
    sent += cd

    if T == 4:
        for h in range(2):
            project(2, h, ps.at[2])
            cp.append(send_sum(2, h, pair, 2))
            cp[h].wait_recv()
            ps[1, :, half_of(h)] = (
                passing[:, half_of(h)] + pr[0, :, half_of(h)].astype(F32)
            ).astype(BF16)
            cp.append(send_sum(1, h, across, 1))
    else:
        for i in range(half, len(far)):
            for h in range(2):
                project(i, h, ps.at[i])
                cp.append(send_sum(i, h, blocks[i], me))
    sent += cp

    for c in cd:
        c.wait_recv()
    total_down = ds[...]
    for k in range(1, T):
        total_down = total_down + dr[lax.rem(me + k, T)]
    down = jnp.concatenate([total_down[:, :RANK], total_down[:, RANK:]], axis=0)
    twice = jnp.concatenate([down, down], axis=1)
    lifted_in = (jnp.concatenate([twice] * (AO * RANK // 128), axis=1) * mask).astype(BF16)
    lifted = jnp.dot(lifted_in, u_b[...], preferred_element_type=F32).astype(BF16)
    for o in range(O):
        rs[o] = lifted[o * CAP:(o + 1) * CAP, :]
    cr = []
    for k in range(1, O):
        o = lax.rem(mo + k, O)
        cr.append(to_owner(k, o, rs.at[o], rr.at[mo], s_r, r_r))
    sent += cr
    rr[mo] = rs[mo]

    for h in range(2):
        project(T - 1, h, own)
    for c in cp[2:] if T == 4 else cp:
        c.wait_recv()
    for c in cr:
        c.wait_recv()
    step = min(512, CB)
    for j in range(CB // step):
        cols = slice(j * step, (j + 1) * step)
        whole = jnp.dot(
            sel_t[...], rr[:, :, cols].reshape(OC, step), preferred_element_type=F32
        )
        base = own[:, cols]
        for i in [1, 2] if T == 4 else [lax.rem(me + k, T) for k in range(1, T)]:
            base = base + pr[i, :, cols].astype(F32)
        out_ref[:, cols] = (base + whole).astype(BF16)
    for c in sent:
        c.wait_send()


def local(mesh, q, k, v, lengths, ra, abr, w, d, u):
    T, O = mesh.shape["tensor"], mesh.shape["owner"]
    R, KB = q.shape
    NR, POS, KW = k.shape
    AO, RANK, CB = u.shape
    CAP = 2 * R // O
    OC = O * CAP
    HT = HQ // T
    TN = min(512, CB // 2)
    vm = pltpu.VMEM
    dma = pltpu.SemaphoreType.DMA
    scratch = [
        vm((NR, POS, KW), BF16), vm((NR, POS, KW), BF16),
        vm((T, KB, CB), BF16),
        vm((AO, RANK, KB), F32), vm((AO, RANK, CB), F32),
        vm((AO * RANK, KB), BF16), vm((AO * RANK, CB), BF16),
        vm((T, HT * NR, HEAD), BF16), vm((T, HT * NR, HEAD), BF16), vm((HQ * NR, HEAD), F32),
        vm((HQ * NR, HEAD), F32), vm((T, HT * NR, HEAD), BF16), vm((T, HT * NR, HEAD), BF16),
        vm((R, KB), F32), vm((R, KB), BF16),
        vm((R, OC), BF16), vm((O, CAP, KB + 128), BF16), vm((O, CAP, KB + 128), BF16),
        vm((OC // 2, 2 * RANK), F32), vm((T, OC // 2, 2 * RANK), F32),
        vm((O, CAP, CB), BF16), vm((O, CAP, CB), BF16),
        vm((T, R, CB), BF16), vm((T, R, CB), BF16), vm((R, CB), F32), vm((R, CB), F32),
        dma((NR,)), dma((NR,)), dma((T,)), dma(()), dma(()),
        dma((T,)), dma((T,)), dma((T,)), dma((T,)), dma((O,)), dma((O,)),
        dma((T,)), dma((T,)), dma((O,)), dma((O,)), dma((2 * T,)), dma((2 * T,)),
    ]
    any_spec = pl.BlockSpec(memory_space=pl.ANY)
    vmem_spec = pl.BlockSpec(memory_space=pltpu.VMEM)
    smem_spec = pl.BlockSpec(memory_space=pltpu.SMEM)
    return pl.pallas_call(
        functools.partial(kernel, T, O, CAP, TN),
        out_shape=jax.ShapeDtypeStruct((R, CB), BF16),
        in_specs=[vmem_spec, smem_spec, vmem_spec, vmem_spec] + [any_spec] * 5,
        out_specs=vmem_spec,
        scratch_shapes=scratch,
        compiler_params=pltpu.CompilerParams(
            collective_id=0, has_side_effects=True, vmem_limit_bytes=60 * 2**20
        ),
        name="attend_project_adapt",
    )(q, lengths, ra.reshape(1, -1), abr.reshape(1, -1), k, v, w, jnp.swapaxes(d, 1, 2), u)


def solution(mesh):
    return jax.shard_map(
        functools.partial(local, mesh),
        mesh=mesh,
        in_specs=(
            P(("groups", "owner"), "tensor"),
            P(("groups", "owner", "tensor"), None, None),
            P(("groups", "owner", "tensor"), None, None),
            P(("groups", "owner", "tensor")),
            P(("groups", "owner")),
            P("groups"),
            P("tensor", None),
            P(("groups", "owner"), "tensor", None),
            P(("groups", "owner"), None, "tensor"),
        ),
        out_specs=P(("groups", "owner"), "tensor"),
        check_vma=False,
    )
```

```python
import functools
import math

import jax
import jax.numpy as jnp
from jax import lax
from jax.experimental import pallas as pl
from jax.experimental.pallas import tpu as pltpu
from jax.sharding import PartitionSpec as P

HQ = 64
KVH = 8
HEAD = 128
F32 = jnp.float32
BF16 = jnp.bfloat16
NT = (((1,), (1,)), ((), ()))


def kernel(
    T, O, CAP, TN,
    q_ref, len_ref, ra_ref, abr_ref, k_hbm, v_hbm, w_hbm, d_hbm, u_hbm,
    out_ref,
    kv_k, kv_v, w_v, d_f, u_f, d_b, u_b,
    qs, qr, qf, attf, atts, attr, xf, xb,
    sel_t, disp, grecv, ds, dr, rs, rr, ps, pr, own, passing,
    lk, lv, lw, ld, lu,
    s_q, r_q, s_a, r_a, s_g, r_g, s_d, r_d, s_r, r_r, s_p, r_p,
):
    me = lax.axis_index("tensor")
    mo = lax.axis_index("owner")
    R, KB = q_ref.shape
    CB = out_ref.shape[1]
    NR = k_hbm.shape[0]
    POS = k_hbm.shape[1]
    HT = HQ // T
    AO, RANK = u_hbm.shape[0], u_hbm.shape[1]
    OC = O * CAP
    far = [(T // 2 + i) % T for i in range(T) if (T // 2 + i) % T != 0]

    loads_k, loads_v = [], []
    for r in range(NR):
        loads_k.append(pltpu.make_async_copy(k_hbm.at[r], kv_k.at[r], lk.at[r]))
        loads_v.append(pltpu.make_async_copy(v_hbm.at[r], kv_v.at[r], lv.at[r]))
        loads_k[r].start()
        loads_v[r].start()
    load_d = pltpu.make_async_copy(d_hbm, d_f, ld)
    load_u = pltpu.make_async_copy(u_hbm, u_f, lu)
    load_d.start()
    load_u.start()
    pair = me + 1 - 2 * lax.rem(me, 2)
    across = lax.rem(me + 2, T)
    if T == 4:
        blocks = [lax.rem(pair + 2, T), across, pair, me]
    else:
        blocks = [lax.rem(me + k, T) for k in far] + [me]
    loads_w = []
    for i, to in enumerate(blocks):
        loads_w.append(pltpu.make_async_copy(
            w_hbm.at[:, pl.ds(pl.multiple_of(to * CB, CB), CB)], w_v.at[i], lw.at[i]
        ))

    def fetch(first, last):
        for i in range(first, min(last, T)):
            loads_w[i].start()


    fetch(0, 2)

    barrier = pltpu.get_barrier_semaphore()
    for k in range(1, T):
        pl.semaphore_signal(barrier, inc=1, device_id={"tensor": lax.rem(me + k, T)})
    for k in range(1, O):
        pl.semaphore_signal(barrier, inc=1, device_id={"owner": lax.rem(mo + k, O)})

    for t in range(T):
        rows = q_ref[t * NR:(t + 1) * NR, :].astype(F32)
        qs[t] = jnp.concatenate(
            [rows[:, h * HEAD:(h + 1) * HEAD] for h in range(HT)], axis=0
        ).astype(BF16)
    pl.semaphore_wait(barrier, T + O - 2)

    def to_device(i, target, src, dst, ss, rs_):
        c = pltpu.make_async_remote_copy(
            src_ref=src, dst_ref=dst, send_sem=ss.at[i], recv_sem=rs_.at[i],
            device_id={"tensor": target},
        )
        c.start()
        return c

    def to_tensor(k, src, dst, ss, rs_):
        return to_device(k, lax.rem(me + k, T), src, dst, ss, rs_)

    def to_owner(k, target, src, dst, ss, rs_):
        c = pltpu.make_async_remote_copy(
            src_ref=src, dst_ref=dst, send_sem=ss.at[k], recv_sem=rs_.at[k],
            device_id={"owner": target},
        )
        c.start()
        return c

    sent = []
    near = sorted(range(1, T), key=lambda k: min(k, T - k))
    cq = {k: to_tensor(k, qs.at[lax.rem(me + k, T)], qr.at[me], s_q, r_q) for k in near}
    sent += cq.values()
    qr[me] = qs[me]

    A = abr_ref.shape[1]
    ia = lax.broadcasted_iota(jnp.int32, (A, A), 0)
    la = lax.broadcasted_iota(jnp.int32, (A, A), 1)
    abr_col = jnp.sum(jnp.where(ia == la, abr_ref[...], 0), axis=1, keepdims=True)
    hits = lax.broadcasted_iota(jnp.int32, (A, R), 0) == ra_ref[...]
    bank = jnp.sum(jnp.where(hits, abr_col, 0), axis=0, keepdims=True)
    who = bank // AO
    inner = bank - who * AO
    OP = max(8, O)
    eq = (lax.broadcasted_iota(jnp.int32, (OP, R), 0) == who).astype(F32)
    ir = lax.broadcasted_iota(jnp.int32, (R, R), 0)
    lr = lax.broadcasted_iota(jnp.int32, (R, R), 1)
    before = jnp.dot(
        eq.astype(BF16), (ir < lr).astype(F32).astype(BF16), preferred_element_type=F32
    )
    rank = jnp.sum(eq * before, axis=0, keepdims=True).astype(jnp.int32)
    place = who * CAP + rank
    sel = (lax.broadcasted_iota(jnp.int32, (OC, R), 0) == place).astype(F32).astype(BF16)
    place_col = jnp.sum(jnp.where(ir == lr, place, 0), axis=1, keepdims=True)
    sel_t[...] = (
        (lax.broadcasted_iota(jnp.int32, (R, OC), 1) == place_col).astype(F32).astype(BF16)
    )
    inner_t = (lax.broadcasted_iota(jnp.int32, (128, R), 0) == inner).astype(F32).astype(BF16)
    marks = lax.dot_general(sel, inner_t, NT, preferred_element_type=F32).astype(BF16)
    for o in range(O):
        disp[o, :, KB:] = marks[o * CAP:(o + 1) * CAP, :]

    G = HQ // KVH
    for c in loads_k + loads_v:
        c.wait()
    KH = max(1, KVH // T)
    rows_of = KH * G
    head_of = lax.broadcasted_iota(jnp.int32, (rows_of, KH * HEAD), 0) // G
    lane_of = lax.broadcasted_iota(jnp.int32, (rows_of, KH * HEAD), 1) // HEAD
    diagonal = head_of == lane_of
    pos = lax.broadcasted_iota(jnp.int32, (rows_of, POS), 1)
    valid = [pos < len_ref[r] for r in range(NR)]
    valid_all = jnp.concatenate(valid, axis=0)

    def attend(first_row, columns):
        scores = []
        for r in range(NR):
            q_r = qf[pl.ds(first_row + r, rows_of, stride=NR), :]
            wide = jnp.where(diagonal, jnp.concatenate([q_r] * KH, axis=1), 0.0).astype(BF16)
            scores.append(
                lax.dot_general(wide, kv_k[r, :, columns], NT, preferred_element_type=F32)
            )
        scores = jnp.concatenate(scores, axis=0) * (1.0 / math.sqrt(HEAD))
        scores = jnp.where(valid_all, scores, -1e30)
        highest = jnp.max(scores, axis=1, keepdims=True)
        expo = jnp.where(valid_all, jnp.exp(scores - highest), 0.0)
        total = jnp.sum(expo, axis=1, keepdims=True)
        weights = expo.astype(BF16)
        for r in range(NR):
            rows = slice(r * rows_of, (r + 1) * rows_of)
            mixed = jnp.dot(weights[rows], kv_v[r, :, columns], preferred_element_type=F32)
            mixed = jnp.concatenate(
                [mixed[g * G:(g + 1) * G, g * HEAD:(g + 1) * HEAD] for g in range(KH)], axis=0
            )
            attf[pl.ds(first_row + r, rows_of, stride=NR), :] = mixed / total[rows]

    BR = HT * NR
    ca = []
    if KVH % T == 0:
        started = 2
        for k in [0] + near:
            d = lax.rem(me + k, T)
            if k:
                cq[T - k].wait_recv()
            first = pl.multiple_of(d * BR, BR)
            qf[pl.ds(first, BR), :] = qr[d].astype(F32)
            attend(first, pl.ds(pl.multiple_of(d * KH * HEAD, KH * HEAD), KH * HEAD))
            atts[d] = attf[pl.ds(first, BR), :].astype(BF16)
            if k:
                ca.append(to_tensor(k, atts.at[d], attr.at[me], s_a, r_a))
            fetch(started, started + 1)
            started += 1
        fetch(started, T)
    else:
        fetch(2, T)
        for c in cq.values():
            c.wait_recv()
        for t in range(T):
            qf[t * BR:(t + 1) * BR, :] = qr[t].astype(F32)
        for g in range(KVH):
            attend(g * G * NR, slice(g * HEAD, (g + 1) * HEAD))
        for t in range(T):
            atts[t] = attf[t * BR:(t + 1) * BR, :].astype(BF16)
        ca = [to_tensor(k, atts.at[lax.rem(me + k, T)], attr.at[me], s_a, r_a) for k in far]
    sent += ca
    attr[me] = atts[me]

    load_d.wait()
    load_u.wait()

    @pl.loop(0, AO)
    def _(a):
        rows = pl.ds(pl.multiple_of(a * RANK, RANK), RANK)
        d_b[rows, :] = d_f[a].astype(BF16)
        u_b[rows, :] = u_f[a].astype(BF16)

    for c in ca:
        c.wait_recv()
    for t in range(T):
        got = attr[t].astype(F32)
        for h in range(HT):
            xf[t * NR:(t + 1) * NR, h * HEAD:(h + 1) * HEAD] = got[h * NR:(h + 1) * NR, :]
    xb[...] = xf[...].astype(BF16)

    disp_rows = jnp.dot(sel, xb[...], preferred_element_type=F32).astype(BF16)
    for o in range(O):
        disp[o, :, :KB] = disp_rows[o * CAP:(o + 1) * CAP, :]
    cg = []
    for k in range(1, O):
        o = lax.rem(mo + k, O)
        cg.append(to_owner(k, o, disp.at[o], grecv.at[mo], s_g, r_g))
    sent += cg
    grecv[mo] = disp[mo]

    HB = CB // 2

    def project(i, h, out):
        if h == 0:
            loads_w[i].wait()

        @pl.loop(0, HB // TN)
        def _(j):
            cols = pl.ds(pl.multiple_of(h * HB + j * TN, TN), TN)
            part = jnp.dot(xb[...], w_v[i, :, cols], preferred_element_type=F32)
            out[:, cols] = part.astype(out.dtype)

    def half_of(h):
        return slice(h * HB, (h + 1) * HB)

    def send_sum(i, h, target, slot):
        return to_device(
            2 * i + h, target, ps.at[i, :, half_of(h)], pr.at[slot, :, half_of(h)], s_p, r_p
        )

    cp = []
    if T == 4:
        for h in range(2):
            project(0, h, ps.at[0])
            cp.append(send_sum(0, h, pair, 0))
        for h in range(2):
            project(1, h, passing)
    else:
        half = len(far) // 3
        for i in range(half):
            for h in range(2):
                project(i, h, ps.at[i])
                cp.append(send_sum(i, h, blocks[i], me))

    for c in cg:
        c.wait_recv()
    rows_in = grecv[...].reshape(OC, KB + 128)
    ej = lax.broadcasted_iota(jnp.int32, (128, AO * RANK), 0)
    el = lax.broadcasted_iota(jnp.int32, (128, AO * RANK), 1) // RANK
    spread = (ej == el).astype(F32).astype(BF16)
    mask = jnp.dot(rows_in[:, KB:], spread, preferred_element_type=F32)
    every = lax.dot_general(rows_in[:, :KB], d_b[...], NT, preferred_element_type=F32) * mask
    lanes = every[:, :128]
    for i in range(1, AO * RANK // 128):
        lanes = lanes + every[:, i * 128:(i + 1) * 128]
    down = lanes[:, :RANK] + lanes[:, RANK:]
    ds[...] = jnp.concatenate([down[:OC // 2], down[OC // 2:]], axis=1)
    cd = [to_tensor(k, ds, dr.at[me], s_d, r_d) for k in far]
    sent += cd

    if T == 4:
        for h in range(2):
            project(2, h, ps.at[2])
            cp.append(send_sum(2, h, pair, 2))
            cp[h].wait_recv()
            ps[1, :, half_of(h)] = (
                passing[:, half_of(h)] + pr[0, :, half_of(h)].astype(F32)
            ).astype(BF16)
            cp.append(send_sum(1, h, across, 1))
    else:
        for i in range(half, len(far)):
            for h in range(2):
                project(i, h, ps.at[i])
                cp.append(send_sum(i, h, blocks[i], me))
    sent += cp

    for c in cd:
        c.wait_recv()
    total_down = ds[...]
    for k in range(1, T):
        total_down = total_down + dr[lax.rem(me + k, T)]
    down = jnp.concatenate([total_down[:, :RANK], total_down[:, RANK:]], axis=0)
    twice = jnp.concatenate([down, down], axis=1)
    lifted_in = (jnp.concatenate([twice] * (AO * RANK // 128), axis=1) * mask).astype(BF16)
    lifted = jnp.dot(lifted_in, u_b[...], preferred_element_type=F32).astype(BF16)
    for o in range(O):
        rs[o] = lifted[o * CAP:(o + 1) * CAP, :]
    cr = []
    for k in range(1, O):
        o = lax.rem(mo + k, O)
        cr.append(to_owner(k, o, rs.at[o], rr.at[mo], s_r, r_r))
    sent += cr
    rr[mo] = rs[mo]

    for h in range(2):
        project(T - 1, h, own)
    for c in cp[2:] if T == 4 else cp:
        c.wait_recv()
    for c in cr:
        c.wait_recv()
    step = min(512, CB)
    for j in range(CB // step):
        cols = slice(j * step, (j + 1) * step)
        whole = jnp.dot(
            sel_t[...], rr[:, :, cols].reshape(OC, step), preferred_element_type=F32
        )
        base = own[:, cols]
        for i in [1, 2] if T == 4 else [lax.rem(me + k, T) for k in range(1, T)]:
            base = base + pr[i, :, cols].astype(F32)
        out_ref[:, cols] = (base + whole).astype(BF16)
    for c in sent:
        c.wait_send()


def local(mesh, q, k, v, lengths, ra, abr, w, d, u):
    T, O = mesh.shape["tensor"], mesh.shape["owner"]
    R, KB = q.shape
    NR, POS, KW = k.shape
    AO, RANK, CB = u.shape
    CAP = 2 * R // O
    OC = O * CAP
    HT = HQ // T
    TN = min(512, CB // 2)
    vm = pltpu.VMEM
    dma = pltpu.SemaphoreType.DMA
    scratch = [
        vm((NR, POS, KW), BF16), vm((NR, POS, KW), BF16),
        vm((T, KB, CB), BF16),
        vm((AO, RANK, KB), F32), vm((AO, RANK, CB), F32),
        vm((AO * RANK, KB), BF16), vm((AO * RANK, CB), BF16),
        vm((T, HT * NR, HEAD), BF16), vm((T, HT * NR, HEAD), BF16), vm((HQ * NR, HEAD), F32),
        vm((HQ * NR, HEAD), F32), vm((T, HT * NR, HEAD), BF16), vm((T, HT * NR, HEAD), BF16),
        vm((R, KB), F32), vm((R, KB), BF16),
        vm((R, OC), BF16), vm((O, CAP, KB + 128), BF16), vm((O, CAP, KB + 128), BF16),
        vm((OC // 2, 2 * RANK), F32), vm((T, OC // 2, 2 * RANK), F32),
        vm((O, CAP, CB), BF16), vm((O, CAP, CB), BF16),
        vm((T, R, CB), BF16), vm((T, R, CB), BF16), vm((R, CB), F32), vm((R, CB), F32),
        dma((NR,)), dma((NR,)), dma((T,)), dma(()), dma(()),
        dma((T,)), dma((T,)), dma((T,)), dma((T,)), dma((O,)), dma((O,)),
        dma((T,)), dma((T,)), dma((O,)), dma((O,)), dma((2 * T,)), dma((2 * T,)),
    ]
    any_spec = pl.BlockSpec(memory_space=pl.ANY)
    vmem_spec = pl.BlockSpec(memory_space=pltpu.VMEM)
    smem_spec = pl.BlockSpec(memory_space=pltpu.SMEM)
    return pl.pallas_call(
        functools.partial(kernel, T, O, CAP, TN),
        out_shape=jax.ShapeDtypeStruct((R, CB), BF16),
        in_specs=[vmem_spec, smem_spec, vmem_spec, vmem_spec] + [any_spec] * 5,
        out_specs=vmem_spec,
        scratch_shapes=scratch,
        compiler_params=pltpu.CompilerParams(
            collective_id=0, has_side_effects=True, vmem_limit_bytes=60 * 2**20
        ),
        name="attend_project_adapt",
    )(q, lengths, ra.reshape(1, -1), abr.reshape(1, -1), k, v, w, jnp.swapaxes(d, 1, 2), u)


def solution(mesh):
    return jax.shard_map(
        functools.partial(local, mesh),
        mesh=mesh,
        in_specs=(
            P(("groups", "owner"), "tensor"),
            P(("groups", "owner", "tensor"), None, None),
            P(("groups", "owner", "tensor"), None, None),
            P(("groups", "owner", "tensor")),
            P(("groups", "owner")),
            P("groups"),
            P("tensor", None),
            P(("groups", "owner"), "tensor", None),
            P(("groups", "owner"), None, "tensor"),
        ),
        out_specs=P(("groups", "owner"), "tensor"),
        check_vma=False,
    )
```

```python
import functools
import math

import jax
import jax.numpy as jnp
from jax import lax
from jax.experimental import pallas as pl
from jax.experimental.pallas import tpu as pltpu
from jax.sharding import PartitionSpec as P

HQ = 64
KVH = 8
HEAD = 128
F32 = jnp.float32
BF16 = jnp.bfloat16
NT = (((1,), (1,)), ((), ()))


def kernel(
    T, O, CAP, TN,
    q_ref, len_ref, ra_ref, abr_ref, k_hbm, v_hbm, w_hbm, d_hbm, u_hbm,
    out_ref,
    kv_k, kv_v, w_v, d_f, u_f, d_b, u_b,
    qs, qr, qf, attf, atts, attr, xf, xb,
    sel_t, disp, grecv, ds, dr, rs, rr, ps, pr, own, passing,
    lk, lv, lw, ld, lu,
    s_q, r_q, s_a, r_a, s_g, r_g, s_d, r_d, s_r, r_r, s_p, r_p,
):
    me = lax.axis_index("tensor")
    mo = lax.axis_index("owner")
    R, KB = q_ref.shape
    CB = out_ref.shape[1]
    NR = k_hbm.shape[0]
    POS = k_hbm.shape[1]
    HT = HQ // T
    AO, RANK = u_hbm.shape[0], u_hbm.shape[1]
    OC = O * CAP
    far = [(T // 2 + i) % T for i in range(T) if (T // 2 + i) % T != 0]

    loads_k, loads_v = [], []
    for r in range(NR):
        loads_k.append(pltpu.make_async_copy(k_hbm.at[r], kv_k.at[r], lk.at[r]))
        loads_v.append(pltpu.make_async_copy(v_hbm.at[r], kv_v.at[r], lv.at[r]))
        loads_k[r].start()
        loads_v[r].start()
    load_d = pltpu.make_async_copy(d_hbm, d_f, ld)
    load_u = pltpu.make_async_copy(u_hbm, u_f, lu)
    load_d.start()
    load_u.start()
    pair = me + 1 - 2 * lax.rem(me, 2)
    across = lax.rem(me + 2, T)
    if T == 4:
        blocks = [lax.rem(pair + 2, T), across, pair, me]
    else:
        blocks = [lax.rem(me + k, T) for k in far] + [me]
    loads_w = []
    for i, to in enumerate(blocks):
        loads_w.append(pltpu.make_async_copy(
            w_hbm.at[:, pl.ds(pl.multiple_of(to * CB, CB), CB)], w_v.at[i], lw.at[i]
        ))

    def fetch(first, last):
        for i in range(first, min(last, T)):
            loads_w[i].start()


    fetch(0, 2)

    barrier = pltpu.get_barrier_semaphore()
    for k in range(1, T):
        pl.semaphore_signal(barrier, inc=1, device_id={"tensor": lax.rem(me + k, T)})
    for k in range(1, O):
        pl.semaphore_signal(barrier, inc=1, device_id={"owner": lax.rem(mo + k, O)})

    for t in range(T):
        rows = q_ref[t * NR:(t + 1) * NR, :].astype(F32)
        qs[t] = jnp.concatenate(
            [rows[:, h * HEAD:(h + 1) * HEAD] for h in range(HT)], axis=0
        ).astype(BF16)
    pl.semaphore_wait(barrier, T + O - 2)

    def to_device(i, target, src, dst, ss, rs_):
        c = pltpu.make_async_remote_copy(
            src_ref=src, dst_ref=dst, send_sem=ss.at[i], recv_sem=rs_.at[i],
            device_id={"tensor": target},
        )
        c.start()
        return c

    def to_tensor(k, src, dst, ss, rs_):
        return to_device(k, lax.rem(me + k, T), src, dst, ss, rs_)

    def to_owner(k, target, src, dst, ss, rs_):
        c = pltpu.make_async_remote_copy(
            src_ref=src, dst_ref=dst, send_sem=ss.at[k], recv_sem=rs_.at[k],
            device_id={"owner": target},
        )
        c.start()
        return c

    sent = []
    near = sorted(range(1, T), key=lambda k: min(k, T - k))
    cq = {k: to_tensor(k, qs.at[lax.rem(me + k, T)], qr.at[me], s_q, r_q) for k in near}
    sent += cq.values()
    qr[me] = qs[me]

    A = abr_ref.shape[1]
    ia = lax.broadcasted_iota(jnp.int32, (A, A), 0)
    la = lax.broadcasted_iota(jnp.int32, (A, A), 1)
    abr_col = jnp.sum(jnp.where(ia == la, abr_ref[...], 0), axis=1, keepdims=True)
    hits = lax.broadcasted_iota(jnp.int32, (A, R), 0) == ra_ref[...]
    bank = jnp.sum(jnp.where(hits, abr_col, 0), axis=0, keepdims=True)
    who = bank // AO
    inner = bank - who * AO
    OP = max(8, O)
    eq = (lax.broadcasted_iota(jnp.int32, (OP, R), 0) == who).astype(F32)
    ir = lax.broadcasted_iota(jnp.int32, (R, R), 0)
    lr = lax.broadcasted_iota(jnp.int32, (R, R), 1)
    before = jnp.dot(
        eq.astype(BF16), (ir < lr).astype(F32).astype(BF16), preferred_element_type=F32
    )
    rank = jnp.sum(eq * before, axis=0, keepdims=True).astype(jnp.int32)
    place = who * CAP + rank
    sel = (lax.broadcasted_iota(jnp.int32, (OC, R), 0) == place).astype(F32).astype(BF16)
    place_col = jnp.sum(jnp.where(ir == lr, place, 0), axis=1, keepdims=True)
    sel_t[...] = (
        (lax.broadcasted_iota(jnp.int32, (R, OC), 1) == place_col).astype(F32).astype(BF16)
    )
    inner_t = (lax.broadcasted_iota(jnp.int32, (128, R), 0) == inner).astype(F32).astype(BF16)
    marks = lax.dot_general(sel, inner_t, NT, preferred_element_type=F32).astype(BF16)
    for o in range(O):
        disp[o, :, KB:] = marks[o * CAP:(o + 1) * CAP, :]

    G = HQ // KVH
    for c in loads_k + loads_v:
        c.wait()
    KH = max(1, KVH // T)
    rows_of = KH * G
    head_of = lax.broadcasted_iota(jnp.int32, (rows_of, KH * HEAD), 0) // G
    lane_of = lax.broadcasted_iota(jnp.int32, (rows_of, KH * HEAD), 1) // HEAD
    diagonal = head_of == lane_of
    pos = lax.broadcasted_iota(jnp.int32, (rows_of, POS), 1)
    valid = [pos < len_ref[r] for r in range(NR)]
    valid_all = jnp.concatenate(valid, axis=0)

    def attend(first_row, columns):
        scores = []
        for r in range(NR):
            q_r = qf[pl.ds(first_row + r, rows_of, stride=NR), :]
            wide = jnp.where(diagonal, jnp.concatenate([q_r] * KH, axis=1), 0.0).astype(BF16)
            scores.append(
                lax.dot_general(wide, kv_k[r, :, columns], NT, preferred_element_type=F32)
            )
        scores = jnp.concatenate(scores, axis=0) * (1.0 / math.sqrt(HEAD))
        scores = jnp.where(valid_all, scores, -1e30)
        highest = jnp.max(scores, axis=1, keepdims=True)
        expo = jnp.where(valid_all, jnp.exp(scores - highest), 0.0)
        total = jnp.sum(expo, axis=1, keepdims=True)
        weights = expo.astype(BF16)
        for r in range(NR):
            rows = slice(r * rows_of, (r + 1) * rows_of)
            mixed = jnp.dot(weights[rows], kv_v[r, :, columns], preferred_element_type=F32)
            mixed = jnp.concatenate(
                [mixed[g * G:(g + 1) * G, g * HEAD:(g + 1) * HEAD] for g in range(KH)], axis=0
            )
            attf[pl.ds(first_row + r, rows_of, stride=NR), :] = mixed / total[rows]

    BR = HT * NR
    ca = []
    if KVH % T == 0:
        started = 2
        for k in [0] + near:
            d = lax.rem(me + k, T)
            if k:
                cq[T - k].wait_recv()
            first = pl.multiple_of(d * BR, BR)
            qf[pl.ds(first, BR), :] = qr[d].astype(F32)
            attend(first, pl.ds(pl.multiple_of(d * KH * HEAD, KH * HEAD), KH * HEAD))
            atts[d] = attf[pl.ds(first, BR), :].astype(BF16)
            if k:
                ca.append(to_tensor(k, atts.at[d], attr.at[me], s_a, r_a))
            fetch(started, started + 1)
            started += 1
        fetch(started, T)
    else:
        fetch(2, T)
        for c in cq.values():
            c.wait_recv()
        for t in range(T):
            qf[t * BR:(t + 1) * BR, :] = qr[t].astype(F32)
        for g in range(KVH):
            attend(g * G * NR, slice(g * HEAD, (g + 1) * HEAD))
        for t in range(T):
            atts[t] = attf[t * BR:(t + 1) * BR, :].astype(BF16)
        ca = [to_tensor(k, atts.at[lax.rem(me + k, T)], attr.at[me], s_a, r_a) for k in far]
    sent += ca
    attr[me] = atts[me]

    load_d.wait()
    load_u.wait()

    @pl.loop(0, AO)
    def _(a):
        rows = pl.ds(pl.multiple_of(a * RANK, RANK), RANK)
        d_b[rows, :] = d_f[a].astype(BF16)
        u_b[rows, :] = u_f[a].astype(BF16)

    for c in ca:
        c.wait_recv()
    for t in range(T):
        got = attr[t].astype(F32)
        for h in range(HT):
            xf[t * NR:(t + 1) * NR, h * HEAD:(h + 1) * HEAD] = got[h * NR:(h + 1) * NR, :]
    xb[...] = xf[...].astype(BF16)

    disp_rows = jnp.dot(sel, xb[...], preferred_element_type=F32).astype(BF16)
    for o in range(O):
        disp[o, :, :KB] = disp_rows[o * CAP:(o + 1) * CAP, :]
    cg = []
    for k in range(1, O):
        o = lax.rem(mo + k, O)
        cg.append(to_owner(k, o, disp.at[o], grecv.at[mo], s_g, r_g))
    sent += cg
    grecv[mo] = disp[mo]

    HB = CB // 2

    def project(i, h, out):
        if h == 0:
            loads_w[i].wait()

        @pl.loop(0, HB // TN)
        def _(j):
            cols = pl.ds(pl.multiple_of(h * HB + j * TN, TN), TN)
            part = jnp.dot(xb[...], w_v[i, :, cols], preferred_element_type=F32)
            out[:, cols] = part.astype(out.dtype)

    def half_of(h):
        return slice(h * HB, (h + 1) * HB)

    def send_sum(i, h, target, slot):
        return to_device(
            2 * i + h, target, ps.at[i, :, half_of(h)], pr.at[slot, :, half_of(h)], s_p, r_p
        )

    cp = []
    if T == 4:
        for h in range(2):
            project(0, h, ps.at[0])
            cp.append(send_sum(0, h, pair, 0))
        for h in range(2):
            project(1, h, passing)
    else:
        half = len(far) // 3
        for i in range(half):
            for h in range(2):
                project(i, h, ps.at[i])
                cp.append(send_sum(i, h, blocks[i], me))

    for c in cg:
        c.wait_recv()
    rows_in = grecv[...].reshape(OC, KB + 128)
    ej = lax.broadcasted_iota(jnp.int32, (128, AO * RANK), 0)
    el = lax.broadcasted_iota(jnp.int32, (128, AO * RANK), 1) // RANK
    spread = (ej == el).astype(F32).astype(BF16)
    mask = jnp.dot(rows_in[:, KB:], spread, preferred_element_type=F32)
    every = lax.dot_general(rows_in[:, :KB], d_b[...], NT, preferred_element_type=F32) * mask
    lanes = every[:, :128]
    for i in range(1, AO * RANK // 128):
        lanes = lanes + every[:, i * 128:(i + 1) * 128]
    down = lanes[:, :RANK] + lanes[:, RANK:]
    ds[...] = jnp.concatenate([down[:OC // 2], down[OC // 2:]], axis=1)
    cd = [to_tensor(k, ds, dr.at[me], s_d, r_d) for k in far]
    sent += cd

    if T == 4:
        for h in range(2):
            cp[h].wait_recv()
            ps[1, :, half_of(h)] = (
                passing[:, half_of(h)] + pr[0, :, half_of(h)].astype(F32)
            ).astype(BF16)
            cp.append(send_sum(1, h, across, 1))
        for h in range(2):
            project(2, h, ps.at[2])
            cp.append(send_sum(2, h, pair, 2))
    else:
        for i in range(half, len(far)):
            for h in range(2):
                project(i, h, ps.at[i])
                cp.append(send_sum(i, h, blocks[i], me))
    sent += cp

    for c in cd:
        c.wait_recv()
    total_down = ds[...]
    for k in range(1, T):
        total_down = total_down + dr[lax.rem(me + k, T)]
    down = jnp.concatenate([total_down[:, :RANK], total_down[:, RANK:]], axis=0)
    twice = jnp.concatenate([down, down], axis=1)
    lifted_in = (jnp.concatenate([twice] * (AO * RANK // 128), axis=1) * mask).astype(BF16)
    lifted = jnp.dot(lifted_in, u_b[...], preferred_element_type=F32).astype(BF16)
    for o in range(O):
        rs[o] = lifted[o * CAP:(o + 1) * CAP, :]
    cr = []
    for k in range(1, O):
        o = lax.rem(mo + k, O)
        cr.append(to_owner(k, o, rs.at[o], rr.at[mo], s_r, r_r))
    sent += cr
    rr[mo] = rs[mo]

    for h in range(2):
        project(T - 1, h, own)
    for c in cp[2:] if T == 4 else cp:
        c.wait_recv()
    for c in cr:
        c.wait_recv()
    step = min(512, CB)
    for j in range(CB // step):
        cols = slice(j * step, (j + 1) * step)
        whole = jnp.dot(
            sel_t[...], rr[:, :, cols].reshape(OC, step), preferred_element_type=F32
        )
        base = own[:, cols]
        for i in [1, 2] if T == 4 else [lax.rem(me + k, T) for k in range(1, T)]:
            base = base + pr[i, :, cols].astype(F32)
        out_ref[:, cols] = (base + whole).astype(BF16)
    for c in sent:
        c.wait_send()


def local(mesh, q, k, v, lengths, ra, abr, w, d, u):
    T, O = mesh.shape["tensor"], mesh.shape["owner"]
    R, KB = q.shape
    NR, POS, KW = k.shape
    AO, RANK, CB = u.shape
    CAP = 2 * R // O
    OC = O * CAP
    HT = HQ // T
    TN = min(512, CB // 2)
    vm = pltpu.VMEM
    dma = pltpu.SemaphoreType.DMA
    scratch = [
        vm((NR, POS, KW), BF16), vm((NR, POS, KW), BF16),
        vm((T, KB, CB), BF16),
        vm((AO, RANK, KB), F32), vm((AO, RANK, CB), F32),
        vm((AO * RANK, KB), BF16), vm((AO * RANK, CB), BF16),
        vm((T, HT * NR, HEAD), BF16), vm((T, HT * NR, HEAD), BF16), vm((HQ * NR, HEAD), F32),
        vm((HQ * NR, HEAD), F32), vm((T, HT * NR, HEAD), BF16), vm((T, HT * NR, HEAD), BF16),
        vm((R, KB), F32), vm((R, KB), BF16),
        vm((R, OC), BF16), vm((O, CAP, KB + 128), BF16), vm((O, CAP, KB + 128), BF16),
        vm((OC // 2, 2 * RANK), F32), vm((T, OC // 2, 2 * RANK), F32),
        vm((O, CAP, CB), BF16), vm((O, CAP, CB), BF16),
        vm((T, R, CB), BF16), vm((T, R, CB), BF16), vm((R, CB), F32), vm((R, CB), F32),
        dma((NR,)), dma((NR,)), dma((T,)), dma(()), dma(()),
        dma((T,)), dma((T,)), dma((T,)), dma((T,)), dma((O,)), dma((O,)),
        dma((T,)), dma((T,)), dma((O,)), dma((O,)), dma((2 * T,)), dma((2 * T,)),
    ]
    any_spec = pl.BlockSpec(memory_space=pl.ANY)
    vmem_spec = pl.BlockSpec(memory_space=pltpu.VMEM)
    smem_spec = pl.BlockSpec(memory_space=pltpu.SMEM)
    return pl.pallas_call(
        functools.partial(kernel, T, O, CAP, TN),
        out_shape=jax.ShapeDtypeStruct((R, CB), BF16),
        in_specs=[vmem_spec, smem_spec, vmem_spec, vmem_spec] + [any_spec] * 5,
        out_specs=vmem_spec,
        scratch_shapes=scratch,
        compiler_params=pltpu.CompilerParams(
            collective_id=0, has_side_effects=True, vmem_limit_bytes=60 * 2**20
        ),
        name="attend_project_adapt",
    )(q, lengths, ra.reshape(1, -1), abr.reshape(1, -1), k, v, w, jnp.swapaxes(d, 1, 2), u)


def solution(mesh):
    return jax.shard_map(
        functools.partial(local, mesh),
        mesh=mesh,
        in_specs=(
            P(("groups", "owner"), "tensor"),
            P(("groups", "owner", "tensor"), None, None),
            P(("groups", "owner", "tensor"), None, None),
            P(("groups", "owner", "tensor")),
            P(("groups", "owner")),
            P("groups"),
            P("tensor", None),
            P(("groups", "owner"), "tensor", None),
            P(("groups", "owner"), None, "tensor"),
        ),
        out_specs=P(("groups", "owner"), "tensor"),
        check_vma=False,
    )
```
